32 devices in a mesh: groups: 2 (over x), row: 16 (over z, y, core).
Axes of the slice: x: 2, y: 2, z: 4, core: 2. Of those that a mesh axis runs over, the one named last changes fastest.
Arguments:
- pair: bfloat16 [256, 128, 128], P(('groups', 'row')), parts along dimension 0, may hold values from -6 to 6
- single: bfloat16 [256, 384], P(('groups', 'row')), parts along dimension 0, may hold values from -6 to 6
- token_mask: int32 [256], P('groups'), parts along dimension 0, may hold values 0 or 1
- chain_index: int32 [256], P('groups'), parts along dimension 0, may hold values from 0 to 7, as said below
- residue_index: int32 [256], P('groups'), parts along dimension 0, may hold values from 0 to 166, as said below
- pair_gain: float32 [128], replicated, may hold values from 0.25 to 1.75
- pair_norm_offset: float32 [128], replicated, may hold values from -3 to 3
- w_swish_a: bfloat16 [128, 512], replicated, may hold values from -0.5 to 0.5
- w_swish_b: bfloat16 [128, 512], replicated, may hold values from -0.5 to 0.5
- w_trans_out: bfloat16 [512, 128], replicated, may hold values from -0.25 to 0.25
- w_pair_bias: bfloat16 [128, 16], replicated, may hold values from -0.5 to 0.5
- w_project: bfloat16 [384, 1536], replicated, may hold values from -0.3125 to 0.3125
- w_out: bfloat16 [384, 384], replicated, may hold values from -0.3125 to 0.3125
- relative_position_bias: float32 [66, 16], replicated, may hold values from -6 to 300
Outputs:
- new_pair: bfloat16 [256, 128, 128], P(('groups', 'row')), parts along dimension 0
- single_update: bfloat16 [256, 384], P(('groups', 'row')), parts along dimension 0
The draws below stay inside these ranges and needn't reach their ends.
There are 2 independent parts, one for each index of `groups`. The reference program is written for one: setup_inputs(seed, part) draws one part's arguments, and reference() takes and returns one part's arrays. A program takes and returns all parts, laid end to end along the dimension named above; an argument that names none is the same for every part. Nothing has to cross between parts.
Inputs may be any that keep to these rules, and one draw needn't show every extreme that they name: `chain_index`: chain numbers never fall along the tokens, start at 0, and every chain 0 to 7 holds one token or more. `residue_index`: within a chain each token's residue number is one more than the previous token's.
All inputs are finite; a program needn't handle non-finite values.
Results may differ from the reference program's by a relative error of at most 0.014.
Values may be sent and summed in bfloat16 or wider, within the bound.
No kernel may reach another device: no remote copies, remote signals or barrier semaphores. Data moves between devices by JAX's collectives and lax.ppermute only.
A program may use at most 64 MiB of HBM per device.

```python
import math
import jax
import jax.numpy as jnp
from jax import lax

C_PAIR = 128
FF = 512
HEADS = 16
HEAD_DIM = 24
D_SINGLE = 384
RELMAX = 32
BINS = 66
CHAINS = 8
TOKENS = 128


def chain_layout(key):
    cut_key = jax.random.fold_in(key, 11)
    shifted_key = jax.random.fold_in(key, 12)
    cuts = jax.random.permutation(cut_key, TOKENS - 1)[:CHAINS - 1] + 1
    starts = jnp.zeros((TOKENS,), jnp.int32).at[cuts].set(1)
    chain = jnp.cumsum(starts).astype(jnp.int32)
    position = jnp.arange(TOKENS, dtype=jnp.int32)
    first = lax.cummax(jnp.where(starts > 0, position, 0), axis=0)
    last_length = (TOKENS - first[TOKENS - 1]).astype(jnp.int32)
    shifts = jax.random.randint(shifted_key, (CHAINS,), 0, 40).astype(jnp.int32)
    shifts = shifts.at[0].set(0).at[CHAINS - 1].set(TOKENS + 39 - last_length)
    residue_number = (position - first + shifts[chain]).astype(jnp.int32)
    return (chain, residue_number)


def draw_chain_index(key, part):
    chain, residue_number = chain_layout(key)
    return chain


def draw_residue_index(key, part):
    chain, residue_number = chain_layout(key)
    return residue_number


def draw_relative_position_bias(key, part):
    base = jnp.clip(jax.random.normal(jax.random.fold_in(key, 21), (BINS, HEADS), jnp.float32), -6.0, 6.0)
    return base


def place_ends(result, stream_key, least, high):
    spot = [jax.random.randint(jax.random.fold_in(stream_key, axis), (), 0, length) for axis, length in enumerate(result.shape)]
    main_axis = result.shape.index(max(result.shape))
    neighbour = spot[:main_axis] + [(spot[main_axis] + 1) % result.shape[main_axis]] + spot[main_axis + 1:]
    return result.at[tuple(spot)].set(least).at[tuple(neighbour)].set(high)


def block_levels(own_key, extent, pieces, least, largest):
    factor_of, own = 1.0, jax.random.fold_in(own_key, 6)
    for dim, parts in pieces:
        heights = jnp.exp(jax.random.uniform(jax.random.fold_in(own, dim), (parts,), jnp.float32, least / len(pieces), largest / len(pieces)))
        factor_of = factor_of * jnp.repeat(heights, extent[dim] // parts).reshape([-1 if axis == dim else 1 for axis in range(len(extent))])
    return factor_of


def scatter_about(key, shape, scale, limit, pieces=(), held_as=jnp.bfloat16):
    drawn = scale * jax.random.normal(key, shape, jnp.float32)
    if pieces:
        drawn = drawn * block_levels(key, shape, pieces, -0.22, 0.18)
    return jnp.clip(drawn, -limit, limit).astype(held_as)


def setup_inputs(seed: int = 0, part: int = 0) -> dict:
    key_of = jax.random.split(jax.random.key(seed), 15)
    own_keys = jax.random.split(jax.random.fold_in(key_of[14], part), 15)
    pair = scatter_about(own_keys[0], (TOKENS, TOKENS, C_PAIR), 1.0, 6.0, ((0, 16),))
    single = scatter_about(own_keys[1], (TOKENS, D_SINGLE), 1.0, 6.0, ((0, 16),))
    token_mask = place_ends((jax.random.randint(own_keys[2], (TOKENS,), 0, 8) < 7).astype(jnp.int32), jax.random.fold_in(own_keys[2], 1), 0, 1)
    chain_index = draw_chain_index(jax.random.fold_in(jax.random.fold_in(key_of[14], part), 71), part)
    residue_index = draw_residue_index(jax.random.fold_in(jax.random.fold_in(key_of[14], part), 71), part)
    pair_gain = jnp.clip(1.0 + 0.15 * jax.random.normal(key_of[5], (C_PAIR,), jnp.float32), 0.25, 1.75)
    pair_norm_offset = scatter_about(key_of[6], (C_PAIR,), 0.5, 3.0, (), jnp.float32)
    w_swish_a = scatter_about(key_of[7], (C_PAIR, FF), C_PAIR ** -0.5, 0.5)
    w_swish_b = scatter_about(key_of[8], (C_PAIR, FF), C_PAIR ** -0.5, 0.5)
    w_trans_out = scatter_about(key_of[9], (FF, C_PAIR), FF ** -0.5, 0.25)
    w_pair_bias = scatter_about(key_of[10], (C_PAIR, HEADS), C_PAIR ** -0.5, 0.5)
    w_project = scatter_about(key_of[11], (D_SINGLE, 4 * D_SINGLE), D_SINGLE ** -0.5, 0.3125)
    w_out = scatter_about(key_of[12], (D_SINGLE, D_SINGLE), D_SINGLE ** -0.5, 0.3125)
    relative_position_bias = draw_relative_position_bias(jax.random.fold_in(key_of[14], 71), part)
    return dict(pair=pair, single=single, token_mask=token_mask, chain_index=chain_index, residue_index=residue_index, pair_gain=pair_gain, pair_norm_offset=pair_norm_offset, w_swish_a=w_swish_a, w_swish_b=w_swish_b, w_trans_out=w_trans_out, w_pair_bias=w_pair_bias, w_project=w_project, w_out=w_out, relative_position_bias=relative_position_bias)


epsilon = 1e-05

def layer_norm(value_rows):
    middle = lax.optimization_barrier(jnp.mean(value_rows, axis=-1, keepdims=True))
    centred = value_rows - middle
    spread = lax.optimization_barrier(jnp.mean(centred * centred, axis=-1, keepdims=True))
    return centred * lax.rsqrt(spread + epsilon)

def relative_bins(res_query, chain_query, res_key, chain_key):
    offset = jnp.clip(res_query[:, None] - res_key[None, :] + RELMAX, 0, 2 * RELMAX)
    return jnp.where(chain_query[:, None] == chain_key[None, :], offset, 2 * RELMAX + 1).astype(jnp.int32)

def transition_row(pair_row, pair_gain, pair_norm_offset, w_swish_a, w_swish_b, w_trans_out):
    normed = (layer_norm(pair_row.astype(jnp.float32)) * pair_gain + pair_norm_offset).astype(jnp.bfloat16)
    first = jnp.dot(normed, w_swish_a, preferred_element_type=jnp.float32)
    second_operand = jnp.dot(normed, w_swish_b, preferred_element_type=jnp.float32)
    hidden = (jax.nn.silu(first) * second_operand).astype(jnp.bfloat16)
    updated = (pair_row.astype(jnp.float32) + jnp.dot(hidden, w_trans_out, preferred_element_type=jnp.float32)).astype(jnp.bfloat16)
    bias_input = layer_norm(updated.astype(jnp.float32)).astype(jnp.bfloat16)
    return (updated, bias_input)

def reference(pair, single, token_mask, chain_index, residue_index, pair_gain, pair_norm_offset, w_swish_a, w_swish_b, w_trans_out, w_pair_bias, w_project, w_out, relative_position_bias):

    def one_row(pair_row):
        updated, bias_input = transition_row(pair_row, pair_gain, pair_norm_offset, w_swish_a, w_swish_b, w_trans_out)
        bias_row = jnp.dot(bias_input, w_pair_bias, preferred_element_type=jnp.float32).astype(jnp.bfloat16)
        return (updated, bias_row)
    new_pair, bias_rows = lax.map(one_row, pair)
    width = HEADS * HEAD_DIM
    normed = layer_norm(single.astype(jnp.float32)).astype(jnp.bfloat16)
    projected = jnp.dot(normed, w_project, preferred_element_type=jnp.float32).astype(jnp.bfloat16)
    queries = projected[:, :width].reshape(TOKENS, HEADS, HEAD_DIM).astype(jnp.float32)
    keys_all = projected[:, width:2 * width].reshape(TOKENS, HEADS, HEAD_DIM).astype(jnp.float32)
    values_all = projected[:, 2 * width:3 * width].reshape(TOKENS, HEADS, HEAD_DIM).astype(jnp.float32)
    gates = projected[:, 3 * width:].astype(jnp.float32)
    scores = jnp.einsum('ihd,jhd->hij', queries, keys_all) / math.sqrt(HEAD_DIM)
    bins = relative_bins(residue_index, chain_index, residue_index, chain_index)
    scores = scores + jnp.transpose(bias_rows.astype(jnp.float32), (2, 0, 1)) + jnp.transpose(relative_position_bias[bins], (2, 0, 1))
    scores = jnp.where(token_mask[None, None, :] > 0, scores, -1000000000.0)
    highest = lax.optimization_barrier(jnp.max(scores, axis=-1, keepdims=True))
    expons = jnp.exp(scores - highest)
    totals = lax.optimization_barrier(jnp.sum(expons, axis=-1))
    weights = lax.optimization_barrier(expons.astype(jnp.bfloat16)).astype(jnp.float32)
    attended_rows = jnp.einsum('hij,jhd->ihd', weights, values_all) / jnp.transpose(totals)[:, :, None]
    gated = (jax.nn.sigmoid(gates) * attended_rows.reshape(TOKENS, width)).astype(jnp.bfloat16)
    single_update = jnp.dot(gated, w_out, preferred_element_type=jnp.float32).astype(jnp.bfloat16)
    return (new_pair, single_update)
```

```python
import functools
import math

import jax
import jax.numpy as jnp
from jax import lax
from jax.experimental import pallas as pl
from jax.experimental.pallas import tpu as pltpu
from jax.sharding import PartitionSpec as P

HEADS = 16
HEAD_DIM = 24
RELMAX = 32
BINS = 66
WIDTH = HEADS * HEAD_DIM
EPSILON = 1e-05
MASKED = -1000000000.0

f32 = jnp.float32
bf16 = jnp.bfloat16
VMEM = pl.BlockSpec(memory_space=pltpu.VMEM)
PARAMS = pltpu.CompilerParams(vmem_limit_bytes=48 * 1024 * 1024)


def layer_norm(rows):
    middle = jnp.mean(rows, axis=-1, keepdims=True)
    centred = rows - middle
    spread = jnp.mean(centred * centred, axis=-1, keepdims=True)
    return centred * lax.rsqrt(spread + EPSILON)


def dot(a, b):
    return jnp.dot(a, b, preferred_element_type=f32)


def dot_nt(a, b):
    return lax.dot_general(a, b, (((1,), (1,)), ((), ())), preferred_element_type=f32)


def head_mask(tokens):
    head = lax.broadcasted_iota(jnp.int32, (tokens, HEADS, WIDTH), 1)
    column = lax.broadcasted_iota(jnp.int32, (tokens, HEADS, WIDTH), 2)
    low = head * HEAD_DIM
    return (column >= low) & (column < low + HEAD_DIM)


def pair_kernel(chunk, pair, gain, shift, w_a, w_b, w_o, w_bias, new_pair, pair_bias):
    rows, tokens, channels = pair.shape
    gains = gain[...][None, :]
    shifts = shift[...][None, :]
    for first in range(0, rows, chunk):
        old = pair[first : first + chunk].reshape(chunk * tokens, channels).astype(f32)
        normed = (layer_norm(old) * gains + shifts).astype(bf16)
        half = dot(normed, w_a[...]) * 0.5
        swish = half + half * jnp.tanh(half)
        hidden = (swish * dot(normed, w_b[...])).astype(bf16)
        updated = (old + dot(hidden, w_o[...])).astype(bf16)
        new_pair[first : first + chunk] = updated.reshape(chunk, tokens, channels)
        bias_input = layer_norm(updated.astype(f32)).astype(bf16)
        for row in range(chunk):
            piece = bias_input[row * tokens : (row + 1) * tokens]
            pair_bias[first + row] = dot_nt(w_bias[...], piece).astype(bf16)


def own_kernel(
    single, w_project, table, chain, residue, mask, pair_bias, queries, gates, added
):
    rows = single.shape[0]
    tokens = chain.shape[0]
    normed = layer_norm(single[...].astype(f32)).astype(bf16)
    query = dot(normed, w_project[:, :WIDTH]).astype(bf16).astype(f32)
    spread = jnp.broadcast_to(query[:, None, :], (rows, HEADS, WIDTH))
    spread = jnp.where(head_mask(rows), spread, 0.0)
    queries[...] = spread.reshape(rows * HEADS, WIDTH).astype(bf16)
    gate = dot(normed, w_project[:, 3 * WIDTH :]).astype(bf16).astype(f32)
    gates[...] = jax.nn.sigmoid(gate)

    first = lax.axis_index("row") * rows
    chain_j = chain[...][None, :]
    residue_j = residue[...][None, :]
    mask_j = mask[...][None, :]
    column = lax.broadcasted_iota(jnp.int32, (rows, tokens), 1)
    own = column == first + lax.broadcasted_iota(jnp.int32, (rows, tokens), 0)
    chain_i = jnp.sum(jnp.where(own, chain_j, 0), axis=1, keepdims=True)
    residue_i = jnp.sum(jnp.where(own, residue_j, 0), axis=1, keepdims=True)
    bins = jnp.clip(residue_i - residue_j + RELMAX, 0, 2 * RELMAX)
    bins = jnp.where(chain_i == chain_j, bins, 2 * RELMAX + 1)
    whole = table[...]
    top = whole.astype(bf16)
    rest = whole - top.astype(f32)
    middle = rest.astype(bf16)
    low = (rest - middle.astype(f32)).astype(bf16)
    pieces = jnp.concatenate([top, middle, low], axis=0)
    classes = lax.broadcasted_iota(jnp.int32, (BINS, tokens), 0)
    for row in range(rows):
        indicator = (classes == bins[row : row + 1]).astype(f32).astype(bf16)
        found = dot(pieces, indicator)
        extra = found[:HEADS] + found[HEADS : 2 * HEADS] + found[2 * HEADS :]
        extra = extra + pair_bias[row].astype(f32)
        added[row] = jnp.where(mask_j > 0, extra, MASKED)


def attend_kernel(
    order, gathered, w_project, queries, gates, added, w_out, update, ordered
):
    rows = gates.shape[0]
    tokens = gathered.shape[0]
    me = lax.axis_index("row")
    arrived = gathered[...].astype(f32)
    for slot, offset in enumerate(order):
        owner = jnp.bitwise_xor(me, offset)
        ordered[pl.ds(pl.multiple_of(owner * rows, rows), rows), :] = arrived[
            slot * rows : (slot + 1) * rows
        ]
    normed = layer_norm(ordered[...]).astype(bf16)
    keys = dot(normed, w_project[:, WIDTH : 2 * WIDTH]).astype(bf16)
    values = dot(normed, w_project[:, 2 * WIDTH : 3 * WIDTH]).astype(bf16)
    extra = added[...].reshape(rows * HEADS, tokens)
    scores = dot_nt(queries[...], keys) * (1.0 / math.sqrt(HEAD_DIM)) + extra
    scores = jnp.where(extra > -100000000.0, scores, MASKED)
    expons = jnp.exp(scores - jnp.max(scores, axis=1, keepdims=True))
    totals = jnp.sum(expons, axis=1, keepdims=True)
    mixed = dot(expons.astype(bf16), values) / totals
    mixed = jnp.where(head_mask(rows), mixed.reshape(rows, HEADS, WIDTH), 0.0)
    gated = (gates[...] * jnp.sum(mixed, axis=1)).astype(bf16)
    update[...] = dot(gated, w_out[...]).astype(bf16)


def gather_rounds(count):
    bits = count.bit_length() - 1
    masks = [(1 << bit) | 1 for bit in range(bits - 1, 0, -1)] + [1]
    if bits < 3:
        return [[m] for m in masks]
    return [[masks[0] ^ masks[1] ^ 1, masks[0], masks[1]]] + [[m] for m in masks[2:]]


def on_device(
    count,
    pair,
    single,
    token_mask,
    chain_index,
    residue_index,
    pair_gain,
    pair_norm_offset,
    w_swish_a,
    w_swish_b,
    w_trans_out,
    w_pair_bias,
    w_project,
    w_out,
    relative_position_bias,
):
    rows, tokens, _ = pair.shape
    width = single.shape[1]
    order = [0]
    gathered = single
    for masks in gather_rounds(count):
        parts = [gathered]
        for mask in masks:
            pairs = [(i, i ^ mask) for i in range(count)]
            parts.append(lax.ppermute(gathered, "row", pairs))
        order = order + [o ^ mask for mask in masks for o in order]
        gathered = jnp.concatenate(parts, axis=0)

    new_pair, pair_bias = pl.pallas_call(
        functools.partial(pair_kernel, max(1, min(rows, 1024 // tokens))),
        out_shape=(
            jax.ShapeDtypeStruct(pair.shape, bf16),
            jax.ShapeDtypeStruct((rows, HEADS, tokens), bf16),
        ),
        in_specs=[VMEM] * 7,
        out_specs=(VMEM, VMEM),
        compiler_params=PARAMS,
        name="pair",
    )(pair, pair_gain, pair_norm_offset, w_swish_a, w_swish_b, w_trans_out, w_pair_bias.T)

    queries, gates, added = pl.pallas_call(
        own_kernel,
        out_shape=(
            jax.ShapeDtypeStruct((rows * HEADS, width), bf16),
            jax.ShapeDtypeStruct((rows, width), f32),
            jax.ShapeDtypeStruct((rows, HEADS, tokens), f32),
        ),
        in_specs=[VMEM] * 7,
        out_specs=(VMEM, VMEM, VMEM),
        compiler_params=PARAMS,
        name="own",
    )(
        single,
        w_project,
        relative_position_bias.T,
        chain_index,
        residue_index,
        token_mask,
        pair_bias,
    )

    update = pl.pallas_call(
        functools.partial(attend_kernel, order),
        out_shape=jax.ShapeDtypeStruct((rows, width), bf16),
        in_specs=[VMEM] * 6,
        out_specs=VMEM,
        scratch_shapes=[pltpu.VMEM((tokens, width), f32)],
        compiler_params=PARAMS,
        name="attend",
    )(gathered, w_project, queries, gates, added, w_out)
    return (new_pair, update)


def solution(mesh):
    return jax.shard_map(
        functools.partial(on_device, mesh.shape["row"]),
        mesh=mesh,
        in_specs=(
            P(("groups", "row"), None, None),
            P(("groups", "row"), None),
            P("groups"),
            P("groups"),
            P("groups"),
            P(),
            P(),
            P(),
            P(),
            P(),
            P(),
            P(),
            P(),
            P(),
        ),
        out_specs=(P(("groups", "row"), None, None), P(("groups", "row"), None)),
        check_vma=False,
    )
```

```python
import functools
import math

import jax
import jax.numpy as jnp
from jax import lax
from jax.experimental import pallas as pl
from jax.experimental.pallas import tpu as pltpu
from jax.sharding import PartitionSpec as P

HEADS = 16
HEAD_DIM = 24
RELMAX = 32
BINS = 66
WIDTH = HEADS * HEAD_DIM
EPSILON = 1e-05
MASKED = -1000000000.0

f32 = jnp.float32
bf16 = jnp.bfloat16
VMEM = pl.BlockSpec(memory_space=pltpu.VMEM)
ANY = pl.BlockSpec(memory_space=pl.ANY)
PARAMS = pltpu.CompilerParams(vmem_limit_bytes=48 * 1024 * 1024)


def layer_norm(rows):
    middle = jnp.mean(rows, axis=-1, keepdims=True)
    centred = rows - middle
    spread = jnp.mean(centred * centred, axis=-1, keepdims=True)
    return centred * lax.rsqrt(spread + EPSILON)


def dot(a, b):
    return jnp.dot(a, b, preferred_element_type=f32)


def dot_nt(a, b):
    return lax.dot_general(a, b, (((1,), (1,)), ((), ())), preferred_element_type=f32)


def head_mask(tokens):
    head = lax.broadcasted_iota(jnp.int32, (tokens, HEADS, WIDTH), 1)
    column = lax.broadcasted_iota(jnp.int32, (tokens, HEADS, WIDTH), 2)
    low = head * HEAD_DIM
    return (column >= low) & (column < low + HEAD_DIM)


def pair_kernel(chunk, *refs):
    (pair, gain, shift, w_a, w_b, w_o, w_bias) = refs[:7]
    later = refs[7:14]
    new_pair, pair_bias = refs[14:16]
    kept = refs[16:23]
    local = refs[23:30]
    sems = refs[30]
    sources = (pair, gain, shift, w_a, w_b, w_o, w_bias) + later
    targets = local + kept
    copies = [
        pltpu.make_async_copy(source, target, sems.at[i])
        for i, (source, target) in enumerate(zip(sources, targets))
    ]
    for copy in copies:
        copy.start()
    pair, gain, shift, w_a, w_b, w_o, w_bias = local
    rows, tokens, channels = pair.shape
    for copy in copies[:7]:
        copy.wait()
    gains = gain[...][None, :]
    shifts = shift[...][None, :]
    for first in range(0, rows, chunk):
        old = pair[first : first + chunk].reshape(chunk * tokens, channels).astype(f32)
        normed = (layer_norm(old) * gains + shifts).astype(bf16)
        half = dot(normed, w_a[...]) * 0.5
        swish = half + half * jnp.tanh(half)
        hidden = (swish * dot(normed, w_b[...])).astype(bf16)
        updated = (old + dot(hidden, w_o[...])).astype(bf16)
        new_pair[first : first + chunk] = updated.reshape(chunk, tokens, channels)
        bias_input = layer_norm(updated.astype(f32)).astype(bf16)
        for row in range(chunk):
            piece = bias_input[row * tokens : (row + 1) * tokens]
            pair_bias[first + row] = dot_nt(w_bias[...], piece).astype(bf16)
    for copy in copies[7:]:
        copy.wait()


def own_kernel(
    single,
    w_project,
    table,
    chain,
    residue,
    mask,
    pair_bias,
    held_pair,
    queries,
    gates,
    added,
    new_pair,
    sem,
):
    copy = pltpu.make_async_copy(held_pair, new_pair, sem)
    copy.start()
    rows = single.shape[0]
    tokens = chain.shape[0]
    normed = layer_norm(single[...].astype(f32)).astype(bf16)
    query = dot(normed, w_project[:, :WIDTH]).astype(bf16).astype(f32)
    spread = jnp.broadcast_to(query[:, None, :], (rows, HEADS, WIDTH))
    spread = jnp.where(head_mask(rows), spread, 0.0)
    queries[...] = spread.reshape(rows * HEADS, WIDTH).astype(bf16)
    gate = dot(normed, w_project[:, 3 * WIDTH :]).astype(bf16).astype(f32)
    gates[...] = jax.nn.sigmoid(gate)

    first = lax.axis_index("row") * rows
    chain_j = chain[...][None, :]
    residue_j = residue[...][None, :]
    mask_j = mask[...][None, :]
    column = lax.broadcasted_iota(jnp.int32, (rows, tokens), 1)
    own = column == first + lax.broadcasted_iota(jnp.int32, (rows, tokens), 0)
    chain_i = jnp.sum(jnp.where(own, chain_j, 0), axis=1, keepdims=True)
    residue_i = jnp.sum(jnp.where(own, residue_j, 0), axis=1, keepdims=True)
    bins = jnp.clip(residue_i - residue_j + RELMAX, 0, 2 * RELMAX)
    bins = jnp.where(chain_i == chain_j, bins, 2 * RELMAX + 1)
    whole = table[...]
    top = whole.astype(bf16)
    rest = whole - top.astype(f32)
    middle = rest.astype(bf16)
    low = (rest - middle.astype(f32)).astype(bf16)
    pieces = jnp.concatenate([top, middle, low], axis=0)
    classes = lax.broadcasted_iota(jnp.int32, (BINS, tokens), 0)
    for row in range(rows):
        indicator = (classes == bins[row : row + 1]).astype(f32).astype(bf16)
        found = dot(pieces, indicator)
        extra = found[:HEADS] + found[HEADS : 2 * HEADS] + found[2 * HEADS :]
        extra = extra + pair_bias[row].astype(f32)
        added[row] = jnp.where(mask_j > 0, extra, MASKED)
    copy.wait()


def attend_kernel(
    order, gathered, w_project, queries, gates, added, w_out, update, ordered
):
    rows = gates.shape[0]
    tokens = gathered.shape[0]
    me = lax.axis_index("row")
    arrived = gathered[...].astype(f32)
    for slot, offset in enumerate(order):
        owner = jnp.bitwise_xor(me, offset)
        ordered[pl.ds(pl.multiple_of(owner * rows, rows), rows), :] = arrived[
            slot * rows : (slot + 1) * rows
        ]
    normed = layer_norm(ordered[...]).astype(bf16)
    keys = dot(normed, w_project[:, WIDTH : 2 * WIDTH]).astype(bf16)
    values = dot(normed, w_project[:, 2 * WIDTH : 3 * WIDTH]).astype(bf16)
    extra = added[...].reshape(rows * HEADS, tokens)
    scores = dot_nt(queries[...], keys) * (1.0 / math.sqrt(HEAD_DIM)) + extra
    scores = jnp.where(extra > -100000000.0, scores, MASKED)
    expons = jnp.exp(scores - jnp.max(scores, axis=1, keepdims=True))
    totals = jnp.sum(expons, axis=1, keepdims=True)
    mixed = dot(expons.astype(bf16), values) / totals
    mixed = jnp.where(head_mask(rows), mixed.reshape(rows, HEADS, WIDTH), 0.0)
    gated = (gates[...] * jnp.sum(mixed, axis=1)).astype(bf16)
    update[...] = dot(gated, w_out[...]).astype(bf16)


def gather_rounds(count):
    bits = count.bit_length() - 1
    masks = [(1 << bit) | 1 for bit in range(bits - 1, 0, -1)] + [1]
    if bits < 3:
        return [[m] for m in masks]
    return [[masks[0] ^ masks[1] ^ 1, masks[0], masks[1]]] + [[m] for m in masks[2:]]


def on_device(
    count,
    pair,
    single,
    token_mask,
    chain_index,
    residue_index,
    pair_gain,
    pair_norm_offset,
    w_swish_a,
    w_swish_b,
    w_trans_out,
    w_pair_bias,
    w_project,
    w_out,
    relative_position_bias,
):
    rows, tokens, _ = pair.shape
    width = single.shape[1]
    operands = (
        pair,
        pair_gain,
        pair_norm_offset,
        w_swish_a,
        w_swish_b,
        w_trans_out,
        w_pair_bias.T,
        single,
        w_project,
        w_out,
        relative_position_bias.T,
        chain_index,
        residue_index,
        token_mask,
    )
    held = pl.pallas_call(
        functools.partial(pair_kernel, max(1, min(rows, 1024 // tokens))),
        out_shape=(
            jax.ShapeDtypeStruct(pair.shape, bf16),
            jax.ShapeDtypeStruct((rows, HEADS, tokens), bf16),
        )
        + tuple(jax.ShapeDtypeStruct(a.shape, a.dtype) for a in operands[7:]),
        in_specs=[ANY] * 14,
        out_specs=(VMEM,) * 9,
        scratch_shapes=[pltpu.VMEM(a.shape, a.dtype) for a in operands[:7]]
        + [pltpu.SemaphoreType.DMA((14,))],
        compiler_params=PARAMS,
        name="pair",
    )(*(pltpu.with_memory_space_constraint(a, pltpu.HBM) for a in operands))
    held_pair, pair_bias, held_single, held_project, held_out = held[:5]
    held_table, held_chain, held_residue, held_mask = held[5:]

    order = [0]
    gathered = single
    own = held_single
    for masks in gather_rounds(count):
        parts = [own]
        for mask in masks:
            pairs = [(i, i ^ mask) for i in range(count)]
            parts.append(lax.ppermute(gathered, "row", pairs))
        order = order + [o ^ mask for mask in masks for o in order]
        gathered = own = jnp.concatenate(parts, axis=0)

    queries, gates, added, new_pair = pl.pallas_call(
        own_kernel,
        out_shape=(
            jax.ShapeDtypeStruct((rows * HEADS, width), bf16),
            jax.ShapeDtypeStruct((rows, width), f32),
            jax.ShapeDtypeStruct((rows, HEADS, tokens), f32),
            jax.ShapeDtypeStruct(pair.shape, bf16),
        ),
        in_specs=[VMEM] * 8,
        out_specs=(VMEM, VMEM, VMEM, ANY),
        scratch_shapes=[pltpu.SemaphoreType.DMA],
        compiler_params=PARAMS,
        name="own",
    )(
        held_single,
        held_project,
        held_table,
        held_chain,
        held_residue,
        held_mask,
        pair_bias,
        held_pair,
    )

    update = pl.pallas_call(
        functools.partial(attend_kernel, order),
        out_shape=jax.ShapeDtypeStruct((rows, width), bf16),
        in_specs=[VMEM] * 6,
        out_specs=VMEM,
        scratch_shapes=[pltpu.VMEM((tokens, width), f32)],
        compiler_params=PARAMS,
        name="attend",
    )(gathered, held_project, queries, gates, added, held_out)
    return (new_pair, update)


def solution(mesh):
    return jax.shard_map(
        functools.partial(on_device, mesh.shape["row"]),
        mesh=mesh,
        in_specs=(
            P(("groups", "row"), None, None),
            P(("groups", "row"), None),
            P("groups"),
            P("groups"),
            P("groups"),
            P(),
            P(),
            P(),
            P(),
            P(),
            P(),
            P(),
            P(),
            P(),
        ),
        out_specs=(P(("groups", "row"), None, None), P(("groups", "row"), None)),
        check_vma=False,
    )
```

```python
import functools
import math

import jax
import jax.numpy as jnp
from jax import lax
from jax.experimental import pallas as pl
from jax.experimental.pallas import tpu as pltpu
from jax.sharding import PartitionSpec as P

HEADS = 16
HEAD_DIM = 24
RELMAX = 32
BINS = 66
WIDTH = HEADS * HEAD_DIM
EPSILON = 1e-05
MASKED = -1000000000.0
EARLY = 6

f32 = jnp.float32
bf16 = jnp.bfloat16
VMEM = pl.BlockSpec(memory_space=pltpu.VMEM)
ANY = pl.BlockSpec(memory_space=pl.ANY)
PARAMS = pltpu.CompilerParams(vmem_limit_bytes=48 * 1024 * 1024)


def layer_norm(rows):
    middle = jnp.mean(rows, axis=-1, keepdims=True)
    centred = rows - middle
    spread = jnp.mean(centred * centred, axis=-1, keepdims=True)
    return centred * lax.rsqrt(spread + EPSILON)


def dot(a, b):
    return jnp.dot(a, b, preferred_element_type=f32)


def dot_nt(a, b):
    return lax.dot_general(a, b, (((1,), (1,)), ((), ())), preferred_element_type=f32)


def head_mask(tokens):
    head = lax.broadcasted_iota(jnp.int32, (tokens, HEADS, WIDTH), 1)
    column = lax.broadcasted_iota(jnp.int32, (tokens, HEADS, WIDTH), 2)
    low = head * HEAD_DIM
    return (column >= low) & (column < low + HEAD_DIM)


def transition(pair, weights, chunk, new_pair, pair_bias, first_bias):
    gain, shift, w_a, w_b, w_o, w_bias = weights
    rows, tokens, channels = pair.shape
    gains = gain[...][None, :]
    shifts = shift[...][None, :]
    for first in range(0, rows, chunk):
        old = pair[first : first + chunk].reshape(chunk * tokens, channels).astype(f32)
        normed = (layer_norm(old) * gains + shifts).astype(bf16)
        half = dot(normed, w_a[...]) * 0.5
        swish = half + half * jnp.tanh(half)
        hidden = (swish * dot(normed, w_b[...])).astype(bf16)
        updated = (old + dot(hidden, w_o[...])).astype(bf16)
        new_pair[first : first + chunk] = updated.reshape(chunk, tokens, channels)
        bias_input = layer_norm(updated.astype(f32)).astype(bf16)
        for row in range(chunk):
            piece = bias_input[row * tokens : (row + 1) * tokens]
            pair_bias[first_bias + first + row] = dot_nt(w_bias[...], piece).astype(bf16)


def early_kernel(early, chunk, *refs):
    sources = refs[:14]
    new_pair, pair_bias, late_pair = refs[14:17]
    kept = refs[17:30]
    early_pair, sems = refs[30:]
    rows = sources[0].shape[0]
    starts = [
        (sources[0].at[pl.ds(0, early)], early_pair),
        *zip(sources[1:7], kept[:6]),
        (sources[0].at[pl.ds(early, rows - early)], late_pair),
        *zip(sources[7:], kept[6:]),
    ]
    copies = [pltpu.make_async_copy(*ends, sems.at[i]) for i, ends in enumerate(starts)]
    for copy in copies:
        copy.start()
    for copy in copies[:7]:
        copy.wait()
    transition(early_pair, kept[:6], chunk, new_pair, pair_bias, 0)
    for copy in copies[7:]:
        copy.wait()


def late_kernel(chunk, *refs):
    weights = refs[:6]
    single, w_project, table, chain, residue, mask = refs[6:12]
    early_pair, early_bias, late_pair, received = refs[12:16]
    queries, gates, added, new_pair, passed = refs[16:21]
    late_new, late_bias, sems = refs[21:]
    early = early_pair.shape[0]
    late = late_pair.shape[0]
    first_copy = pltpu.make_async_copy(early_pair, new_pair.at[pl.ds(0, early)], sems.at[0])
    first_copy.start()
    passed[...] = received[...]
    transition(late_pair, weights, chunk, late_new, late_bias, 0)
    copy = pltpu.make_async_copy(late_new, new_pair.at[pl.ds(early, late)], sems.at[1])
    copy.start()

    rows = single.shape[0]
    tokens = chain.shape[0]
    normed = layer_norm(single[...].astype(f32)).astype(bf16)
    query = dot(normed, w_project[:, :WIDTH]).astype(bf16).astype(f32)
    spread = jnp.broadcast_to(query[:, None, :], (rows, HEADS, WIDTH))
    spread = jnp.where(head_mask(rows), spread, 0.0)
    queries[...] = spread.reshape(rows * HEADS, WIDTH).astype(bf16)
    gate = dot(normed, w_project[:, 3 * WIDTH :]).astype(bf16).astype(f32)
    gates[...] = jax.nn.sigmoid(gate)

    first = lax.axis_index("row") * rows
    chain_j = chain[...][None, :]
    residue_j = residue[...][None, :]
    mask_j = mask[...][None, :]
    column = lax.broadcasted_iota(jnp.int32, (rows, tokens), 1)
    own = column == first + lax.broadcasted_iota(jnp.int32, (rows, tokens), 0)
    chain_i = jnp.sum(jnp.where(own, chain_j, 0), axis=1, keepdims=True)
    residue_i = jnp.sum(jnp.where(own, residue_j, 0), axis=1, keepdims=True)
    bins = jnp.clip(residue_i - residue_j + RELMAX, 0, 2 * RELMAX)
    bins = jnp.where(chain_i == chain_j, bins, 2 * RELMAX + 1)
    whole = table[...]
    top = whole.astype(bf16)
    rest = whole - top.astype(f32)
    middle = rest.astype(bf16)
    low = (rest - middle.astype(f32)).astype(bf16)
    pieces = jnp.concatenate([top, middle, low], axis=0)
    classes = lax.broadcasted_iota(jnp.int32, (BINS, tokens), 0)
    for row in range(rows):
        indicator = (classes == bins[row : row + 1]).astype(f32).astype(bf16)
        found = dot(pieces, indicator)
        extra = found[:HEADS] + found[HEADS : 2 * HEADS] + found[2 * HEADS :]
        bias = early_bias[row] if row < early else late_bias[row - early]
        extra = extra + bias.astype(f32)
        added[row] = jnp.where(mask_j > 0, extra, MASKED)
    first_copy.wait()
    copy.wait()


def attend_kernel(
    order, gathered, w_project, queries, gates, added, w_out, update, ordered
):
    rows = gates.shape[0]
    tokens = gathered.shape[0]
    me = lax.axis_index("row")
    arrived = gathered[...].astype(f32)
    for slot, offset in enumerate(order):
        owner = jnp.bitwise_xor(me, offset)
        ordered[pl.ds(pl.multiple_of(owner * rows, rows), rows), :] = arrived[
            slot * rows : (slot + 1) * rows
        ]
    normed = layer_norm(ordered[...]).astype(bf16)
    keys = dot(normed, w_project[:, WIDTH : 2 * WIDTH]).astype(bf16)
    values = dot(normed, w_project[:, 2 * WIDTH : 3 * WIDTH]).astype(bf16)
    extra = added[...].reshape(rows * HEADS, tokens)
    scores = dot_nt(queries[...], keys) * (1.0 / math.sqrt(HEAD_DIM)) + extra
    scores = jnp.where(extra > -100000000.0, scores, MASKED)
    expons = jnp.exp(scores - jnp.max(scores, axis=1, keepdims=True))
    totals = jnp.sum(expons, axis=1, keepdims=True)
    mixed = dot(expons.astype(bf16), values) / totals
    mixed = jnp.where(head_mask(rows), mixed.reshape(rows, HEADS, WIDTH), 0.0)
    gated = (gates[...] * jnp.sum(mixed, axis=1)).astype(bf16)
    update[...] = dot(gated, w_out[...]).astype(bf16)


def chunk_of(rows, tokens):
    return max(d for d in range(1, rows + 1) if rows % d == 0 and (d == 1 or d * tokens <= 1024))


def gather_rounds(count):
    bits = count.bit_length() - 1
    masks = [(1 << bit) | 1 for bit in range(bits - 1, 0, -1)] + [1]
    if bits < 3:
        return [[m] for m in masks]
    return [[masks[0], masks[1], masks[0] ^ masks[1] ^ 1]] + [[m] for m in masks[2:]]


def on_device(
    count,
    pair,
    single,
    token_mask,
    chain_index,
    residue_index,
    pair_gain,
    pair_norm_offset,
    w_swish_a,
    w_swish_b,
    w_trans_out,
    w_pair_bias,
    w_project,
    w_out,
    relative_position_bias,
):
    rows, tokens, _ = pair.shape
    width = single.shape[1]
    operands = (
        pair,
        pair_gain,
        pair_norm_offset,
        w_swish_a,
        w_swish_b,
        w_trans_out,
        w_pair_bias.T,
        single,
        w_project,
        w_out,
        relative_position_bias.T,
        chain_index,
        residue_index,
        token_mask,
    )
    early = max(1, EARLY * rows // 8)
    late = rows - early
    held = pl.pallas_call(
        functools.partial(early_kernel, early, chunk_of(early, tokens)),
        out_shape=(
            jax.ShapeDtypeStruct((early,) + pair.shape[1:], bf16),
            jax.ShapeDtypeStruct((early, HEADS, tokens), bf16),
            jax.ShapeDtypeStruct((late,) + pair.shape[1:], bf16),
        )
        + tuple(jax.ShapeDtypeStruct(a.shape, a.dtype) for a in operands[1:]),
        in_specs=[ANY] * 14,
        out_specs=(VMEM,) * 16,
        scratch_shapes=[
            pltpu.VMEM((early,) + pair.shape[1:], bf16),
            pltpu.SemaphoreType.DMA((15,)),
        ],
        compiler_params=PARAMS,
        name="early",
    )(*(pltpu.with_memory_space_constraint(a, pltpu.HBM) for a in operands))
    early_pair, early_bias, late_pair = held[:3]
    weights = held[3:9]
    held_single, held_project, held_out = held[9:12]
    places = held[12:16]

    order = [0]
    gathered = single
    own = held_single
    for step, masks in enumerate(gather_rounds(count)):
        parts = [own]
        for mask in masks:
            pairs = [(i, i ^ mask) for i in range(count)]
            parts.append(lax.ppermute(gathered, "row", pairs))
        if step == 1:
            queries, gates, added, new_pair, parts[0] = pl.pallas_call(
                functools.partial(late_kernel, chunk_of(late, tokens)),
                out_shape=(
                    jax.ShapeDtypeStruct((rows * HEADS, width), bf16),
                    jax.ShapeDtypeStruct((rows, width), f32),
                    jax.ShapeDtypeStruct((rows, HEADS, tokens), f32),
                    jax.ShapeDtypeStruct(pair.shape, bf16),
                    jax.ShapeDtypeStruct(own.shape, own.dtype),
                ),
                in_specs=[VMEM] * 16,
                out_specs=(VMEM, VMEM, VMEM, ANY, VMEM),
                scratch_shapes=[
                    pltpu.VMEM((late,) + pair.shape[1:], bf16),
                    pltpu.VMEM((late, HEADS, tokens), bf16),
                    pltpu.SemaphoreType.DMA((2,)),
                ],
                compiler_params=PARAMS,
                name="late",
            )(
                *weights,
                held_single,
                held_project,
                *places,
                early_pair,
                early_bias,
                late_pair,
                own,
            )
        order = order + [o ^ mask for mask in masks for o in order]
        gathered = own = jnp.concatenate(parts, axis=0)

    update = pl.pallas_call(
        functools.partial(attend_kernel, order),
        out_shape=jax.ShapeDtypeStruct((rows, width), bf16),
        in_specs=[VMEM] * 6,
        out_specs=VMEM,
        scratch_shapes=[pltpu.VMEM((tokens, width), f32)],
        compiler_params=PARAMS,
        name="attend",
    )(gathered, held_project, queries, gates, added, held_out)
    return (new_pair, update)


def solution(mesh):
    return jax.shard_map(
        functools.partial(on_device, mesh.shape["row"]),
        mesh=mesh,
        in_specs=(
            P(("groups", "row"), None, None),
            P(("groups", "row"), None),
            P("groups"),
            P("groups"),
            P("groups"),
            P(),
            P(),
            P(),
            P(),
            P(),
            P(),
            P(),
            P(),
            P(),
        ),
        out_specs=(P(("groups", "row"), None, None), P(("groups", "row"), None)),
        check_vma=False,
    )
```

```python
import functools
import math

import jax
import jax.numpy as jnp
from jax import lax
from jax.experimental import pallas as pl
from jax.experimental.pallas import tpu as pltpu
from jax.sharding import PartitionSpec as P

HEADS = 16
HEAD_DIM = 24
RELMAX = 32
BINS = 66
WIDTH = HEADS * HEAD_DIM
EPSILON = 1e-05
MASKED = -1000000000.0
EARLY = 6

f32 = jnp.float32
bf16 = jnp.bfloat16
VMEM = pl.BlockSpec(memory_space=pltpu.VMEM)
ANY = pl.BlockSpec(memory_space=pl.ANY)
PARAMS = pltpu.CompilerParams(vmem_limit_bytes=48 * 1024 * 1024)


def layer_norm(rows):
    middle = jnp.mean(rows, axis=-1, keepdims=True)
    centred = rows - middle
    spread = jnp.mean(centred * centred, axis=-1, keepdims=True)
    return centred * lax.rsqrt(spread + EPSILON)


def dot(a, b):
    return jnp.dot(a, b, preferred_element_type=f32)


def dot_nt(a, b):
    return lax.dot_general(a, b, (((1,), (1,)), ((), ())), preferred_element_type=f32)


def head_mask(tokens):
    head = lax.broadcasted_iota(jnp.int32, (tokens, HEADS, WIDTH), 1)
    column = lax.broadcasted_iota(jnp.int32, (tokens, HEADS, WIDTH), 2)
    low = head * HEAD_DIM
    return (column >= low) & (column < low + HEAD_DIM)


def transition(pair, weights, chunk, new_pair, pair_bias, first_bias):
    gain, shift, w_a, w_b, w_o, w_bias = weights
    rows, tokens, channels = pair.shape
    gains = gain[...][None, :]
    shifts = shift[...][None, :]
    for first in range(0, rows, chunk):
        old = pair[first : first + chunk].reshape(chunk * tokens, channels).astype(f32)
        normed = (layer_norm(old) * gains + shifts).astype(bf16)
        half = dot(normed, w_a[...]) * 0.5
        swish = half + half * jnp.tanh(half)
        hidden = (swish * dot(normed, w_b[...])).astype(bf16)
        updated = (old + dot(hidden, w_o[...])).astype(bf16)
        new_pair[first : first + chunk] = updated.reshape(chunk, tokens, channels)
        bias_input = layer_norm(updated.astype(f32)).astype(bf16)
        for row in range(chunk):
            piece = bias_input[row * tokens : (row + 1) * tokens]
            pair_bias[first_bias + first + row] = dot_nt(w_bias[...], piece).astype(bf16)


def early_kernel(early, chunk, *refs):
    sources = refs[:14]
    new_pair, pair_bias, late_pair = refs[14:17]
    kept = refs[17:30]
    early_pair, sems = refs[30:]
    rows = sources[0].shape[0]
    starts = [
        (sources[0].at[pl.ds(0, early)], early_pair),
        *zip(sources[1:7], kept[:6]),
        (sources[0].at[pl.ds(early, rows - early)], late_pair),
        *zip(sources[7:], kept[6:]),
    ]
    copies = [pltpu.make_async_copy(*ends, sems.at[i]) for i, ends in enumerate(starts)]
    for copy in copies:
        copy.start()
    for copy in copies[:7]:
        copy.wait()
    transition(early_pair, kept[:6], chunk, new_pair, pair_bias, 0)
    for copy in copies[7:]:
        copy.wait()


def late_kernel(chunk, *refs):
    weights = refs[:6]
    single, w_project, table, chain, residue, mask = refs[6:12]
    early_pair, early_bias, late_pair, received = refs[12:16]
    queries, gates, added, new_pair, passed = refs[16:21]
    late_new, late_bias, sems = refs[21:]
    early = early_pair.shape[0]
    late = late_pair.shape[0]
    first_copy = pltpu.make_async_copy(early_pair, new_pair.at[pl.ds(0, early)], sems.at[0])
    first_copy.start()
    passed[...] = received[...]
    transition(late_pair, weights, chunk, late_new, late_bias, 0)
    copy = pltpu.make_async_copy(late_new, new_pair.at[pl.ds(early, late)], sems.at[1])
    copy.start()

    rows = single.shape[0]
    tokens = chain.shape[0]
    normed = layer_norm(single[...].astype(f32)).astype(bf16)
    query = dot(normed, w_project[:, :WIDTH]).astype(bf16).astype(f32)
    spread = jnp.broadcast_to(query[:, None, :], (rows, HEADS, WIDTH))
    spread = jnp.where(head_mask(rows), spread, 0.0)
    queries[...] = spread.reshape(rows * HEADS, WIDTH).astype(bf16)
    gate = dot(normed, w_project[:, 3 * WIDTH :]).astype(bf16).astype(f32)
    gates[...] = jax.nn.sigmoid(gate)

    first = lax.axis_index("row") * rows
    chain_j = chain[...][None, :]
    residue_j = residue[...][None, :]
    mask_j = mask[...][None, :]
    column = lax.broadcasted_iota(jnp.int32, (rows, tokens), 1)
    own = column == first + lax.broadcasted_iota(jnp.int32, (rows, tokens), 0)
    chain_i = jnp.sum(jnp.where(own, chain_j, 0), axis=1, keepdims=True)
    residue_i = jnp.sum(jnp.where(own, residue_j, 0), axis=1, keepdims=True)
    bins = jnp.clip(residue_i - residue_j + RELMAX, 0, 2 * RELMAX)
    bins = jnp.where(chain_i == chain_j, bins, 2 * RELMAX + 1)
    whole = table[...]
    top = whole.astype(bf16)
    rest = whole - top.astype(f32)
    middle = rest.astype(bf16)
    low = (rest - middle.astype(f32)).astype(bf16)
    pieces = jnp.concatenate([top, middle, low], axis=0)
    classes = lax.broadcasted_iota(jnp.int32, (BINS, tokens), 0)
    for row in range(rows):
        indicator = (classes == bins[row : row + 1]).astype(f32).astype(bf16)
        found = dot(pieces, indicator)
        extra = found[:HEADS] + found[HEADS : 2 * HEADS] + found[2 * HEADS :]
        bias = early_bias[row] if row < early else late_bias[row - early]
        extra = extra + bias.astype(f32)
        added[row] = jnp.where(mask_j > 0, extra, MASKED)
    first_copy.wait()
    copy.wait()


def attend_kernel(
    order, gathered, w_project, queries, gates, added, w_out, update, ordered
):
    rows = gates.shape[0]
    tokens = gathered.shape[0]
    me = lax.axis_index("row")
    arrived = gathered[...].astype(f32)
    for slot, (table, shift, offset) in enumerate(order):
        packed = sum(source << (2 * place) for place, source in enumerate(table))
        high = lax.shift_right_logical(me, shift)
        source = lax.shift_right_logical(jnp.int32(packed), 2 * high) & 3
        low = jnp.bitwise_xor(me & ((1 << shift) - 1), offset)
        owner = (source << shift) + low
        ordered[pl.ds(pl.multiple_of(owner * rows, rows), rows), :] = arrived[
            slot * rows : (slot + 1) * rows
        ]
    normed = layer_norm(ordered[...]).astype(bf16)
    keys = dot(normed, w_project[:, WIDTH : 2 * WIDTH]).astype(bf16)
    values = dot(normed, w_project[:, 2 * WIDTH : 3 * WIDTH]).astype(bf16)
    extra = added[...].reshape(rows * HEADS, tokens)
    scores = dot_nt(queries[...], keys) * (1.0 / math.sqrt(HEAD_DIM)) + extra
    scores = jnp.where(extra > -100000000.0, scores, MASKED)
    expons = jnp.exp(scores - jnp.max(scores, axis=1, keepdims=True))
    totals = jnp.sum(expons, axis=1, keepdims=True)
    mixed = dot(expons.astype(bf16), values) / totals
    mixed = jnp.where(head_mask(rows), mixed.reshape(rows, HEADS, WIDTH), 0.0)
    gated = (gates[...] * jnp.sum(mixed, axis=1)).astype(bf16)
    update[...] = dot(gated, w_out[...]).astype(bf16)


def chunk_of(rows, tokens):
    return max(d for d in range(1, rows + 1) if rows % d == 0 and (d == 1 or d * tokens <= 1024))


SAME = (0, 1, 2, 3)
QUARTERS = ((2, 3, 1, 0), (1, 0, 3, 2), (3, 2, 0, 1))


def gather_rounds(count):
    shift = count.bit_length() - 3
    rounds = [[(q, 1 if shift else 0) for q in QUARTERS]]
    rounds += [[(SAME, (1 << bit) | 1)] for bit in range(shift - 1, 0, -1)]
    return shift, rounds + ([[(SAME, 1)]] if shift else [])


def on_device(
    count,
    pair,
    single,
    token_mask,
    chain_index,
    residue_index,
    pair_gain,
    pair_norm_offset,
    w_swish_a,
    w_swish_b,
    w_trans_out,
    w_pair_bias,
    w_project,
    w_out,
    relative_position_bias,
):
    rows, tokens, _ = pair.shape
    width = single.shape[1]
    operands = (
        pair,
        pair_gain,
        pair_norm_offset,
        w_swish_a,
        w_swish_b,
        w_trans_out,
        w_pair_bias.T,
        single,
        w_project,
        w_out,
        relative_position_bias.T,
        chain_index,
        residue_index,
        token_mask,
    )
    early = max(1, EARLY * rows // 8)
    late = rows - early
    held = pl.pallas_call(
        functools.partial(early_kernel, early, chunk_of(early, tokens)),
        out_shape=(
            jax.ShapeDtypeStruct((early,) + pair.shape[1:], bf16),
            jax.ShapeDtypeStruct((early, HEADS, tokens), bf16),
            jax.ShapeDtypeStruct((late,) + pair.shape[1:], bf16),
        )
        + tuple(jax.ShapeDtypeStruct(a.shape, a.dtype) for a in operands[1:]),
        in_specs=[ANY] * 14,
        out_specs=(VMEM,) * 16,
        scratch_shapes=[
            pltpu.VMEM((early,) + pair.shape[1:], bf16),
            pltpu.SemaphoreType.DMA((15,)),
        ],
        compiler_params=PARAMS,
        name="early",
    )(*(pltpu.with_memory_space_constraint(a, pltpu.HBM) for a in operands))
    early_pair, early_bias, late_pair = held[:3]
    weights = held[3:9]
    held_single, held_project, held_out = held[9:12]
    places = held[12:16]

    shift, rounds = gather_rounds(count)
    order = [(SAME, shift, 0)]
    gathered = single
    own = held_single
    for step, moves in enumerate(rounds):
        parts = [own]
        slots = list(order)
        for targets, mask in moves:
            pairs = [
                (i, (targets[i >> shift] << shift) + ((i % (1 << shift)) ^ mask))
                for i in range(count)
            ]
            parts.append(lax.ppermute(gathered, "row", pairs))
            for table, _, offset in order:
                sources = table if targets == SAME else tuple(targets.index(q) for q in SAME)
                slots.append((sources, shift, offset ^ mask))
        if step == 1:
            queries, gates, added, new_pair, parts[0] = pl.pallas_call(
                functools.partial(late_kernel, chunk_of(late, tokens)),
                out_shape=(
                    jax.ShapeDtypeStruct((rows * HEADS, width), bf16),
                    jax.ShapeDtypeStruct((rows, width), f32),
                    jax.ShapeDtypeStruct((rows, HEADS, tokens), f32),
                    jax.ShapeDtypeStruct(pair.shape, bf16),
                    jax.ShapeDtypeStruct(own.shape, own.dtype),
                ),
                in_specs=[VMEM] * 16,
                out_specs=(VMEM, VMEM, VMEM, ANY, VMEM),
                scratch_shapes=[
                    pltpu.VMEM((late,) + pair.shape[1:], bf16),
                    pltpu.VMEM((late, HEADS, tokens), bf16),
                    pltpu.SemaphoreType.DMA((2,)),
                ],
                compiler_params=PARAMS,
                name="late",
            )(
                *weights,
                held_single,
                held_project,
                *places,
                early_pair,
                early_bias,
                late_pair,
                own,
            )
        order = slots
        gathered = own = jnp.concatenate(parts, axis=0)

    update = pl.pallas_call(
        functools.partial(attend_kernel, order),
        out_shape=jax.ShapeDtypeStruct((rows, width), bf16),
        in_specs=[VMEM] * 6,
        out_specs=VMEM,
        scratch_shapes=[pltpu.VMEM((tokens, width), f32)],
        compiler_params=PARAMS,
        name="attend",
    )(gathered, held_project, queries, gates, added, held_out)
    return (new_pair, update)


def solution(mesh):
    return jax.shard_map(
        functools.partial(on_device, mesh.shape["row"]),
        mesh=mesh,
        in_specs=(
            P(("groups", "row"), None, None),
            P(("groups", "row"), None),
            P("groups"),
            P("groups"),
            P("groups"),
            P(),
            P(),
            P(),
            P(),
            P(),
            P(),
            P(),
            P(),
            P(),
        ),
        out_specs=(P(("groups", "row"), None, None), P(("groups", "row"), None)),
        check_vma=False,
    )
```

```python
import functools
import math

import jax
import jax.numpy as jnp
from jax import lax
from jax.experimental import pallas as pl
from jax.experimental.pallas import tpu as pltpu
from jax.sharding import PartitionSpec as P

HEADS = 16
HEAD_DIM = 24
RELMAX = 32
BINS = 66
WIDTH = HEADS * HEAD_DIM
EPSILON = 1e-05
MASKED = -1000000000.0
EARLY = 6

f32 = jnp.float32
bf16 = jnp.bfloat16
VMEM = pl.BlockSpec(memory_space=pltpu.VMEM)
ANY = pl.BlockSpec(memory_space=pl.ANY)
PARAMS = pltpu.CompilerParams(vmem_limit_bytes=48 * 1024 * 1024)


def layer_norm(rows):
    middle = jnp.mean(rows, axis=-1, keepdims=True)
    centred = rows - middle
    spread = jnp.mean(centred * centred, axis=-1, keepdims=True)
    return centred * lax.rsqrt(spread + EPSILON)


def dot(a, b):
    return jnp.dot(a, b, preferred_element_type=f32)


def dot_nt(a, b):
    return lax.dot_general(a, b, (((1,), (1,)), ((), ())), preferred_element_type=f32)


def head_mask(tokens):
    head = lax.broadcasted_iota(jnp.int32, (tokens, HEADS, WIDTH), 1)
    column = lax.broadcasted_iota(jnp.int32, (tokens, HEADS, WIDTH), 2)
    low = head * HEAD_DIM
    return (column >= low) & (column < low + HEAD_DIM)


def transition(pair, weights, chunk, new_pair, pair_bias, first_bias):
    gain, shift, w_a, w_b, w_o, w_bias = weights
    rows, tokens, channels = pair.shape
    gains = gain[...][None, :]
    shifts = shift[...][None, :]
    for first in range(0, rows, chunk):
        old = pair[first : first + chunk].reshape(chunk * tokens, channels).astype(f32)
        normed = (layer_norm(old) * gains + shifts).astype(bf16)
        half = dot(normed, w_a[...]) * 0.5
        swish = half + half * jnp.tanh(half)
        hidden = (swish * dot(normed, w_b[...])).astype(bf16)
        updated = (old + dot(hidden, w_o[...])).astype(bf16)
        new_pair[first : first + chunk] = updated.reshape(chunk, tokens, channels)
        bias_input = layer_norm(updated.astype(f32)).astype(bf16)
        for row in range(chunk):
            piece = bias_input[row * tokens : (row + 1) * tokens]
            pair_bias[first_bias + first + row] = dot_nt(w_bias[...], piece).astype(bf16)


def early_kernel(early, chunk, *refs):
    sources = refs[:14]
    new_pair, pair_bias, late_pair = refs[14:17]
    kept = refs[17:30]
    early_pair, sems = refs[30:]
    rows = sources[0].shape[0]
    starts = [
        (sources[0].at[pl.ds(0, early)], early_pair),
        *zip(sources[1:7], kept[:6]),
        (sources[0].at[pl.ds(early, rows - early)], late_pair),
        *zip(sources[7:], kept[6:]),
    ]
    copies = [pltpu.make_async_copy(*ends, sems.at[i]) for i, ends in enumerate(starts)]
    for copy in copies:
        copy.start()
    for copy in copies[:7]:
        copy.wait()
    transition(early_pair, kept[:6], chunk, new_pair, pair_bias, 0)
    for copy in copies[7:]:
        copy.wait()


def late_kernel(chunk, *refs):
    weights = refs[:6]
    single, w_project, table, chain, residue, mask = refs[6:12]
    early_pair, early_bias, late_pair, received = refs[12:16]
    queries, gates, added, sums, new_pair, passed = refs[16:22]
    late_new, late_bias, sems = refs[22:]
    early = early_pair.shape[0]
    late = late_pair.shape[0]
    first_copy = pltpu.make_async_copy(early_pair, new_pair.at[pl.ds(0, early)], sems.at[0])
    first_copy.start()
    passed[...] = received[...]
    transition(late_pair, weights, chunk, late_new, late_bias, 0)
    copy = pltpu.make_async_copy(late_new, new_pair.at[pl.ds(early, late)], sems.at[1])
    copy.start()

    rows = single.shape[0]
    tokens = chain.shape[0]
    normed = layer_norm(single[...].astype(f32)).astype(bf16)
    query = dot(normed, w_project[:, :WIDTH]).astype(bf16).astype(f32)
    spread = jnp.broadcast_to(query[:, None, :], (rows, HEADS, WIDTH))
    spread = jnp.where(head_mask(rows), spread, 0.0)
    queries[...] = spread.reshape(rows * HEADS, WIDTH).astype(bf16)
    gate = dot(normed, w_project[:, 3 * WIDTH :]).astype(bf16).astype(f32)
    gates[...] = jax.nn.sigmoid(gate)
    sums[...] = dot(jnp.ones_like(normed), w_project[:, WIDTH : 3 * WIDTH])

    first = lax.axis_index("row") * rows
    chain_j = chain[...][None, :]
    residue_j = residue[...][None, :]
    mask_j = mask[...][None, :]
    column = lax.broadcasted_iota(jnp.int32, (rows, tokens), 1)
    own = column == first + lax.broadcasted_iota(jnp.int32, (rows, tokens), 0)
    chain_i = jnp.sum(jnp.where(own, chain_j, 0), axis=1, keepdims=True)
    residue_i = jnp.sum(jnp.where(own, residue_j, 0), axis=1, keepdims=True)
    bins = jnp.clip(residue_i - residue_j + RELMAX, 0, 2 * RELMAX)
    bins = jnp.where(chain_i == chain_j, bins, 2 * RELMAX + 1)
    whole = table[...]
    top = whole.astype(bf16)
    rest = whole - top.astype(f32)
    middle = rest.astype(bf16)
    low = (rest - middle.astype(f32)).astype(bf16)
    pieces = jnp.concatenate([top, middle, low], axis=0)
    classes = lax.broadcasted_iota(jnp.int32, (BINS, tokens), 0)
    for row in range(rows):
        indicator = (classes == bins[row : row + 1]).astype(f32).astype(bf16)
        found = dot(pieces, indicator)
        extra = found[:HEADS] + found[HEADS : 2 * HEADS] + found[2 * HEADS :]
        bias = early_bias[row] if row < early else late_bias[row - early]
        extra = extra + bias.astype(f32)
        added[row] = jnp.where(mask_j > 0, extra, MASKED)
    first_copy.wait()
    copy.wait()


def attend_kernel(
    order, known, new, w_project, sums, queries, gates, added, w_out, update, ordered
):
    rows = gates.shape[0]
    tokens = ordered.shape[0]
    me = lax.axis_index("row")
    arrived = (known[...].astype(f32), new[...].astype(f32))
    half = known.shape[0] // rows
    for slot, (table, shift, offset) in enumerate(order):
        packed = sum(source << (2 * place) for place, source in enumerate(table))
        high = lax.shift_right_logical(me, shift)
        source = lax.shift_right_logical(jnp.int32(packed), 2 * high) & 3
        low = jnp.bitwise_xor(me & ((1 << shift) - 1), offset)
        owner = (source << shift) + low
        place = slot % half
        ordered[pl.ds(pl.multiple_of(owner * rows, rows), rows), :] = arrived[slot // half][
            place * rows : (place + 1) * rows
        ]
    single = ordered[...]
    raw = dot(single.astype(bf16), w_project[:, WIDTH : 3 * WIDTH])
    middle = jnp.mean(single, axis=-1, keepdims=True)
    centred = single - middle
    spread = jnp.mean(centred * centred, axis=-1, keepdims=True)
    both = ((raw - middle * sums[0:1, :]) * lax.rsqrt(spread + EPSILON)).astype(bf16)
    keys = both[:, :WIDTH]
    values = both[:, WIDTH:]
    extra = added[...].reshape(rows * HEADS, tokens)
    scores = dot_nt(queries[...], keys) * (1.0 / math.sqrt(HEAD_DIM)) + extra
    scores = jnp.where(extra > -100000000.0, scores, MASKED)
    expons = jnp.exp(scores - jnp.max(scores, axis=1, keepdims=True))
    totals = jnp.sum(expons, axis=1, keepdims=True)
    mixed = dot(expons.astype(bf16), values) * (1.0 / totals)
    mixed = jnp.where(head_mask(rows), mixed.reshape(rows, HEADS, WIDTH), 0.0)
    gated = (gates[...] * jnp.sum(mixed, axis=1)).astype(bf16)
    update[...] = dot(gated, w_out[...]).astype(bf16)


def chunk_of(rows, tokens):
    return max(d for d in range(1, rows + 1) if rows % d == 0 and (d == 1 or d * tokens <= 1024))


SAME = (0, 1, 2, 3)
QUARTERS = ((2, 3, 1, 0), (1, 0, 3, 2), (3, 2, 0, 1))


def gather_rounds(count):
    shift = count.bit_length() - 3
    rounds = [[(q, 1 if shift else 0) for q in QUARTERS]]
    rounds += [[(SAME, (1 << bit) | 1)] for bit in range(shift - 1, 0, -1)]
    return shift, rounds + ([[(SAME, 1)]] if shift else [])


def on_device(
    count,
    pair,
    single,
    token_mask,
    chain_index,
    residue_index,
    pair_gain,
    pair_norm_offset,
    w_swish_a,
    w_swish_b,
    w_trans_out,
    w_pair_bias,
    w_project,
    w_out,
    relative_position_bias,
):
    rows, tokens, _ = pair.shape
    width = single.shape[1]
    operands = (
        pair,
        pair_gain,
        pair_norm_offset,
        w_swish_a,
        w_swish_b,
        w_trans_out,
        w_pair_bias.T,
        single,
        w_project,
        w_out,
        relative_position_bias.T,
        chain_index,
        residue_index,
        token_mask,
    )
    early = max(1, EARLY * rows // 8)
    late = rows - early
    held = pl.pallas_call(
        functools.partial(early_kernel, early, chunk_of(early, tokens)),
        out_shape=(
            jax.ShapeDtypeStruct((early,) + pair.shape[1:], bf16),
            jax.ShapeDtypeStruct((early, HEADS, tokens), bf16),
            jax.ShapeDtypeStruct((late,) + pair.shape[1:], bf16),
        )
        + tuple(jax.ShapeDtypeStruct(a.shape, a.dtype) for a in operands[1:]),
        in_specs=[ANY] * 14,
        out_specs=(VMEM,) * 16,
        scratch_shapes=[
            pltpu.VMEM((early,) + pair.shape[1:], bf16),
            pltpu.SemaphoreType.DMA((15,)),
        ],
        compiler_params=PARAMS,
        name="early",
    )(*(pltpu.with_memory_space_constraint(a, pltpu.HBM) for a in operands))
    early_pair, early_bias, late_pair = held[:3]
    weights = held[3:9]
    held_single, held_project, held_out = held[9:12]
    places = held[12:16]

    shift, rounds = gather_rounds(count)
    order = [(SAME, shift, 0)]
    gathered = single
    own = held_single
    for step, moves in enumerate(rounds):
        parts = [own]
        slots = list(order)
        for targets, mask in moves:
            pairs = [
                (i, (targets[i >> shift] << shift) + ((i % (1 << shift)) ^ mask))
                for i in range(count)
            ]
            parts.append(lax.ppermute(gathered, "row", pairs))
            for table, _, offset in order:
                sources = table if targets == SAME else tuple(targets.index(q) for q in SAME)
                slots.append((sources, shift, offset ^ mask))
        if step == 1:
            queries, gates, added, sums, new_pair, parts[0] = pl.pallas_call(
                functools.partial(late_kernel, chunk_of(late, tokens)),
                out_shape=(
                    jax.ShapeDtypeStruct((rows * HEADS, width), bf16),
                    jax.ShapeDtypeStruct((rows, width), f32),
                    jax.ShapeDtypeStruct((rows, HEADS, tokens), f32),
                    jax.ShapeDtypeStruct((rows, 2 * WIDTH), f32),
                    jax.ShapeDtypeStruct(pair.shape, bf16),
                    jax.ShapeDtypeStruct(own.shape, own.dtype),
                ),
                in_specs=[VMEM] * 16,
                out_specs=(VMEM, VMEM, VMEM, VMEM, ANY, VMEM),
                scratch_shapes=[
                    pltpu.VMEM((late,) + pair.shape[1:], bf16),
                    pltpu.VMEM((late, HEADS, tokens), bf16),
                    pltpu.SemaphoreType.DMA((2,)),
                ],
                compiler_params=PARAMS,
                name="late",
            )(
                *weights,
                held_single,
                held_project,
                *places,
                early_pair,
                early_bias,
                late_pair,
                own,
            )
        order = slots
        gathered = own = jnp.concatenate(parts, axis=0)

    update = pl.pallas_call(
        functools.partial(attend_kernel, order),
        out_shape=jax.ShapeDtypeStruct((rows, width), bf16),
        in_specs=[VMEM] * 8,
        out_specs=VMEM,
        scratch_shapes=[pltpu.VMEM((tokens, width), f32)],
        compiler_params=PARAMS,
        name="attend",
    )(*parts, held_project, sums, queries, gates, added, held_out)
    return (new_pair, update)


def solution(mesh):
    return jax.shard_map(
        functools.partial(on_device, mesh.shape["row"]),
        mesh=mesh,
        in_specs=(
            P(("groups", "row"), None, None),
            P(("groups", "row"), None),
            P("groups"),
            P("groups"),
            P("groups"),
            P(),
            P(),
            P(),
            P(),
            P(),
            P(),
            P(),
            P(),
            P(),
        ),
        out_specs=(P(("groups", "row"), None, None), P(("groups", "row"), None)),
        check_vma=False,
    )
```

```python
import functools
import math

import jax
import jax.numpy as jnp
from jax import lax
from jax.experimental import pallas as pl
from jax.experimental.pallas import tpu as pltpu
from jax.sharding import PartitionSpec as P

HEADS = 16
HEAD_DIM = 24
RELMAX = 32
BINS = 66
WIDTH = HEADS * HEAD_DIM
EPSILON = 1e-05
MASKED = -1000000000.0
EARLY = 5

f32 = jnp.float32
bf16 = jnp.bfloat16
VMEM = pl.BlockSpec(memory_space=pltpu.VMEM)
ANY = pl.BlockSpec(memory_space=pl.ANY)
PARAMS = pltpu.CompilerParams(vmem_limit_bytes=48 * 1024 * 1024)


def layer_norm(rows):
    middle = jnp.mean(rows, axis=-1, keepdims=True)
    centred = rows - middle
    spread = jnp.mean(centred * centred, axis=-1, keepdims=True)
    return centred * lax.rsqrt(spread + EPSILON)


def dot(a, b):
    return jnp.dot(a, b, preferred_element_type=f32)


def dot_nt(a, b):
    return lax.dot_general(a, b, (((1,), (1,)), ((), ())), preferred_element_type=f32)


def head_mask(tokens):
    head = lax.broadcasted_iota(jnp.int32, (tokens, HEADS, WIDTH), 1)
    column = lax.broadcasted_iota(jnp.int32, (tokens, HEADS, WIDTH), 2)
    low = head * HEAD_DIM
    return (column >= low) & (column < low + HEAD_DIM)


def transition(pair, weights, chunk, new_pair, pair_bias, first_bias):
    gain, shift, w_a, w_b, w_o, w_bias = weights
    rows, tokens, channels = pair.shape
    gains = gain[...][None, :]
    shifts = shift[...][None, :]
    for first in range(0, rows, chunk):
        old = pair[first : first + chunk].reshape(chunk * tokens, channels).astype(f32)
        normed = (layer_norm(old) * gains + shifts).astype(bf16)
        half = dot(normed, w_a[...]) * 0.5
        swish = half + half * jnp.tanh(half)
        hidden = (swish * dot(normed, w_b[...])).astype(bf16)
        updated = (old + dot(hidden, w_o[...])).astype(bf16)
        new_pair[first : first + chunk] = updated.reshape(chunk, tokens, channels)
        bias_input = layer_norm(updated.astype(f32)).astype(bf16)
        for row in range(chunk):
            piece = bias_input[row * tokens : (row + 1) * tokens]
            pair_bias[first_bias + first + row] = dot_nt(w_bias[...], piece).astype(bf16)


def early_kernel(early, chunk, *refs):
    sources = refs[:14]
    new_pair, pair_bias, late_pair = refs[14:17]
    kept = refs[17:30]
    early_pair, sems = refs[30:]
    rows = sources[0].shape[0]
    starts = [
        (sources[0].at[pl.ds(0, early)], early_pair),
        *zip(sources[1:7], kept[:6]),
        (sources[0].at[pl.ds(early, rows - early)], late_pair),
        *zip(sources[7:], kept[6:]),
    ]
    copies = [pltpu.make_async_copy(*ends, sems.at[i]) for i, ends in enumerate(starts)]
    for copy in copies:
        copy.start()
    for copy in copies[:7]:
        copy.wait()
    transition(early_pair, kept[:6], chunk, new_pair, pair_bias, 0)
    for copy in copies[7:]:
        copy.wait()


def late_kernel(chunk, *refs):
    weights = refs[:6]
    single, w_project, table, chain, residue, mask = refs[6:12]
    early_pair, early_bias, late_pair, received = refs[12:16]
    queries, gates, added, new_pair, passed = refs[16:21]
    late_new, late_bias, sems = refs[21:]
    early = early_pair.shape[0]
    late = late_pair.shape[0]
    first_copy = pltpu.make_async_copy(early_pair, new_pair.at[pl.ds(0, early)], sems.at[0])
    first_copy.start()
    passed[...] = received[...]
    transition(late_pair, weights, chunk, late_new, late_bias, 0)
    copy = pltpu.make_async_copy(late_new, new_pair.at[pl.ds(early, late)], sems.at[1])
    copy.start()

    rows = single.shape[0]
    tokens = chain.shape[0]
    normed = layer_norm(single[...].astype(f32)).astype(bf16)
    query = dot(normed, w_project[:, :WIDTH]).astype(bf16).astype(f32)
    spread = jnp.broadcast_to(query[:, None, :], (rows, HEADS, WIDTH))
    spread = jnp.where(head_mask(rows), spread, 0.0)
    queries[...] = spread.reshape(rows * HEADS, WIDTH).astype(bf16)
    gate = dot(normed, w_project[:, 3 * WIDTH :]).astype(bf16).astype(f32)
    gates[...] = jax.nn.sigmoid(gate)

    first = lax.axis_index("row") * rows
    chain_j = chain[...][None, :]
    residue_j = residue[...][None, :]
    mask_j = mask[...][None, :]
    column = lax.broadcasted_iota(jnp.int32, (rows, tokens), 1)
    own = column == first + lax.broadcasted_iota(jnp.int32, (rows, tokens), 0)
    chain_i = jnp.sum(jnp.where(own, chain_j, 0), axis=1, keepdims=True)
    residue_i = jnp.sum(jnp.where(own, residue_j, 0), axis=1, keepdims=True)
    bins = jnp.clip(residue_i - residue_j + RELMAX, 0, 2 * RELMAX)
    bins = jnp.where(chain_i == chain_j, bins, 2 * RELMAX + 1)
    whole = table[...]
    top = whole.astype(bf16)
    rest = whole - top.astype(f32)
    middle = rest.astype(bf16)
    low = (rest - middle.astype(f32)).astype(bf16)
    pieces = jnp.concatenate([top, middle, low], axis=0)
    classes = lax.broadcasted_iota(jnp.int32, (BINS, tokens), 0)
    for row in range(rows):
        indicator = (classes == bins[row : row + 1]).astype(f32).astype(bf16)
        found = dot(pieces, indicator)
        extra = found[:HEADS] + found[HEADS : 2 * HEADS] + found[2 * HEADS :]
        bias = early_bias[row] if row < early else late_bias[row - early]
        extra = extra + bias.astype(f32)
        added[row] = jnp.where(mask_j > 0, extra, MASKED)
    first_copy.wait()
    copy.wait()


def attend_kernel(
    order, known, new, w_project, queries, gates, added, w_out, update, ordered
):
    rows = gates.shape[0]
    tokens = ordered.shape[0]
    me = lax.axis_index("row")
    arrived = (known[...].astype(f32), new[...].astype(f32))
    half = known.shape[0] // rows
    for slot, (table, shift, offset) in enumerate(order):
        packed = sum(source << (2 * place) for place, source in enumerate(table))
        high = lax.shift_right_logical(me, shift)
        source = lax.shift_right_logical(jnp.int32(packed), 2 * high) & 3
        low = jnp.bitwise_xor(me & ((1 << shift) - 1), offset)
        owner = (source << shift) + low
        place = slot % half
        ordered[pl.ds(pl.multiple_of(owner * rows, rows), rows), :] = arrived[slot // half][
            place * rows : (place + 1) * rows
        ]
    single = ordered[...]
    ones = jnp.ones((16, WIDTH), bf16)
    raw = dot(
        jnp.concatenate([single.astype(bf16), ones], axis=0), w_project[:, WIDTH : 3 * WIDTH]
    )
    sums = raw[tokens : tokens + 1]
    raw = raw[:tokens]
    middle = jnp.mean(single, axis=-1, keepdims=True)
    centred = single - middle
    spread = jnp.mean(centred * centred, axis=-1, keepdims=True)
    both = ((raw - middle * sums) * lax.rsqrt(spread + EPSILON)).astype(bf16)
    keys = both[:, :WIDTH]
    values = both[:, WIDTH:]
    extra = added[...].reshape(rows * HEADS, tokens)
    scores = dot_nt(queries[...], keys) * (1.0 / math.sqrt(HEAD_DIM)) + extra
    scores = jnp.where(extra > -100000000.0, scores, MASKED)
    expons = jnp.exp(scores - jnp.max(scores, axis=1, keepdims=True))
    totals = jnp.sum(expons, axis=1, keepdims=True)
    mixed = dot(expons.astype(bf16), values) * (1.0 / totals)
    mixed = jnp.where(head_mask(rows), mixed.reshape(rows, HEADS, WIDTH), 0.0)
    gated = (gates[...] * jnp.sum(mixed, axis=1)).astype(bf16)
    update[...] = dot(gated, w_out[...]).astype(bf16)


def chunk_of(rows, tokens):
    return max(d for d in range(1, rows + 1) if rows % d == 0 and (d == 1 or d * tokens <= 1024))


SAME = (0, 1, 2, 3)
QUARTERS = ((2, 3, 1, 0), (1, 0, 3, 2), (3, 2, 0, 1))


def gather_rounds(count):
    shift = count.bit_length() - 3
    rounds = [[(q, 1 if shift else 0) for q in QUARTERS]]
    rounds += [[(SAME, (1 << bit) | 1)] for bit in range(shift - 1, 0, -1)]
    return shift, rounds + ([[(SAME, 1)]] if shift else [])


def on_device(
    count,
    pair,
    single,
    token_mask,
    chain_index,
    residue_index,
    pair_gain,
    pair_norm_offset,
    w_swish_a,
    w_swish_b,
    w_trans_out,
    w_pair_bias,
    w_project,
    w_out,
    relative_position_bias,
):
    rows, tokens, _ = pair.shape
    width = single.shape[1]
    operands = (
        pair,
        pair_gain,
        pair_norm_offset,
        w_swish_a,
        w_swish_b,
        w_trans_out,
        w_pair_bias.T,
        single,
        w_project,
        w_out,
        relative_position_bias.T,
        chain_index,
        residue_index,
        token_mask,
    )
    early = max(1, EARLY * rows // 8)
    late = rows - early
    held = pl.pallas_call(
        functools.partial(early_kernel, early, chunk_of(early, tokens)),
        out_shape=(
            jax.ShapeDtypeStruct((early,) + pair.shape[1:], bf16),
            jax.ShapeDtypeStruct((early, HEADS, tokens), bf16),
            jax.ShapeDtypeStruct((late,) + pair.shape[1:], bf16),
        )
        + tuple(jax.ShapeDtypeStruct(a.shape, a.dtype) for a in operands[1:]),
        in_specs=[ANY] * 14,
        out_specs=(VMEM,) * 16,
        scratch_shapes=[
            pltpu.VMEM((early,) + pair.shape[1:], bf16),
            pltpu.SemaphoreType.DMA((15,)),
        ],
        compiler_params=PARAMS,
        name="early",
    )(*(pltpu.with_memory_space_constraint(a, pltpu.HBM) for a in operands))
    early_pair, early_bias, late_pair = held[:3]
    weights = held[3:9]
    held_single, held_project, held_out = held[9:12]
    places = held[12:16]

    shift, rounds = gather_rounds(count)
    order = [(SAME, shift, 0)]
    gathered = single
    own = held_single
    for step, moves in enumerate(rounds):
        parts = [own]
        slots = list(order)
        for targets, mask in moves:
            pairs = [
                (i, (targets[i >> shift] << shift) + ((i % (1 << shift)) ^ mask))
                for i in range(count)
            ]
            parts.append(lax.ppermute(gathered, "row", pairs))
            for table, _, offset in order:
                sources = table if targets == SAME else tuple(targets.index(q) for q in SAME)
                slots.append((sources, shift, offset ^ mask))
        if step == 1:
            queries, gates, added, new_pair, parts[0] = pl.pallas_call(
                functools.partial(late_kernel, chunk_of(late, tokens)),
                out_shape=(
                    jax.ShapeDtypeStruct((rows * HEADS, width), bf16),
                    jax.ShapeDtypeStruct((rows, width), f32),
                    jax.ShapeDtypeStruct((rows, HEADS, tokens), f32),
                    jax.ShapeDtypeStruct(pair.shape, bf16),
                    jax.ShapeDtypeStruct(own.shape, own.dtype),
                ),
                in_specs=[VMEM] * 16,
                out_specs=(VMEM, VMEM, VMEM, ANY, VMEM),
                scratch_shapes=[
                    pltpu.VMEM((late,) + pair.shape[1:], bf16),
                    pltpu.VMEM((late, HEADS, tokens), bf16),
                    pltpu.SemaphoreType.DMA((2,)),
                ],
                compiler_params=PARAMS,
                name="late",
            )(
                *weights,
                held_single,
                held_project,
                *places,
                early_pair,
                early_bias,
                late_pair,
                own,
            )
        order = slots
        gathered = own = jnp.concatenate(parts, axis=0)

    update = pl.pallas_call(
        functools.partial(attend_kernel, order),
        out_shape=jax.ShapeDtypeStruct((rows, width), bf16),
        in_specs=[VMEM] * 7,
        out_specs=VMEM,
        scratch_shapes=[pltpu.VMEM((tokens, width), f32)],
        compiler_params=PARAMS,
        name="attend",
    )(*parts, held_project, queries, gates, added, held_out)
    return (new_pair, update)


def solution(mesh):
    return jax.shard_map(
        functools.partial(on_device, mesh.shape["row"]),
        mesh=mesh,
        in_specs=(
            P(("groups", "row"), None, None),
            P(("groups", "row"), None),
            P("groups"),
            P("groups"),
            P("groups"),
            P(),
            P(),
            P(),
            P(),
            P(),
            P(),
            P(),
            P(),
            P(),
        ),
        out_specs=(P(("groups", "row"), None, None), P(("groups", "row"), None)),
        check_vma=False,
    )
```
